32 devices in a mesh: rows: 8 (over z, y), grp: 4 (over x, core).
Axes of the slice: x: 2, y: 2, z: 4, core: 2. Of those that a mesh axis runs over, the one named last changes fastest.
Arguments:
- tiles: float32 [1536, 128, 128], P(('rows', 'grp')), may hold values from 0 to 24
- coords: int32 [1536, 2], P(('rows', 'grp')), may hold values from 0 to 127, as said below
- live: int32 [32], P(('rows', 'grp')), may hold values from 6 to 48, as said below
- sketch: float32 [16384, 64], P(('rows', 'grp')), may hold values from -6 to 6
Outputs:
- basis: float32 [16384, 64], P(('rows', 'grp'))
The draws below stay inside these ranges and needn't reach their ends.
Inputs may be any that keep to these rules, and one draw needn't show every extreme that they name: `coords`: slot s of device d (slot d * 48 + s) has the row tile d * 4 + s and the column tile equal to it for s < 4; every other slot of device d has a row tile from d * 4 to d * 4 + 3, and a column tile in row block b - 1, b or b + 1 (modulo 8), where b = d // 4 and row block b is the tiles b * 16 to b * 16 + 15; slot 4 has its column tile in row block b - 1 and slot 5 in row block b + 1. The same coordinate pair may repeat. `live`: every device uses its slots 4 and 5; some device uses all 48.
All inputs are finite; a program needn't handle non-finite values.
Results may differ from the reference program's by a relative error of at most 0.0003.
Values sent between devices are 32-bit elements; how exact they have to be, the bound alone decides.
A program may use at most 64 MiB of HBM per device.

```python
import math
import jax
import jax.numpy as jnp
from jax import lax

TILE = 128
K = 64
TPD = 4
CAP = 48
NROWS = 16384
N_ROWS = 8
N_GRP = 4
DEVICES = 32


def slot_layout(key):
    slot_ids = jnp.arange(DEVICES * CAP, dtype=jnp.int32)
    device = slot_ids // CAP
    within = slot_ids % CAP
    own_row = device * TPD + jax.random.randint(jax.random.fold_in(key, 21), (DEVICES * CAP,), 0, TPD)
    row_tile = jnp.where(within < TPD, device * TPD + within, own_row)
    step_off = jax.random.randint(jax.random.fold_in(key, 22), (DEVICES * CAP,), -1, 2)
    step_off = jnp.where(within == TPD, -1, jnp.where(within == TPD + 1, 1, step_off))
    col_block = (device // N_GRP + step_off + N_ROWS) % N_ROWS
    col_pick = jax.random.randint(jax.random.fold_in(key, 23), (DEVICES * CAP,), 0, N_GRP * TPD)
    col_tile = jnp.where(within < TPD, row_tile, col_block * N_GRP * TPD + col_pick)
    return jnp.stack([row_tile, col_tile], axis=1).astype(jnp.int32)


def slot_counts(key):
    levels = jax.random.randint(jax.random.fold_in(key, 31), (DEVICES,), 0, 16)
    counts = TPD + 2 + (CAP - TPD - 2) * levels * levels * levels // 4096
    fullest = jax.random.randint(jax.random.fold_in(key, 32), (), 0, DEVICES)
    return jnp.where(jnp.arange(DEVICES, dtype=jnp.int32) == fullest, CAP, counts).astype(jnp.int32)


def hub_profile(key):
    ratio_top = 6.0
    lift = 0.86 * ratio_top ** 0.25 * (2.0 * math.log(ratio_top) * NROWS / K) ** 0.125
    ordering = jax.random.permutation(jax.random.fold_in(key, 53), NROWS).astype(jnp.float32)
    falling = jnp.exp(-ordering * (math.log(ratio_top) / (4.0 * K)))
    return jnp.minimum(lift * falling, 4.5)


def node_weights(key):
    ramp = jnp.arange(NROWS, dtype=jnp.float32) / NROWS
    hubs = hub_profile(key)
    rough = jax.random.uniform(jax.random.fold_in(key, 52), (NROWS,), jnp.float32, -0.15, 0.15)
    jitter = jax.random.uniform(jax.random.fold_in(key, 54), (NROWS,), jnp.float32, -0.05, 0.05)
    return jnp.maximum(jnp.exp(-0.4 + 0.4 * ramp + rough), hubs * jnp.exp(jitter))


def draw_coords(key, part):
    return slot_layout(key)


def draw_live(key, part):
    return slot_counts(key)


def draw_tiles(key, part):
    shape = (DEVICES * CAP, TILE, TILE)
    spots = slot_layout(key)
    weights = node_weights(key).reshape(DEVICES * TPD, TILE)
    row_weight = weights[spots[:, 0]]
    col_weight = weights[spots[:, 1]]
    noise = jax.random.uniform(jax.random.fold_in(key, 41), shape, jnp.float32, 0.0, 1.0)
    within = jnp.arange(DEVICES * CAP, dtype=jnp.int32) % CAP
    diagonal = (within < TPD)[:, None, None]
    eye_tile = jnp.eye(TILE, dtype=jnp.float32)[None, :, :]
    near = 0.6 * eye_tile + noise * (1.0 / TILE)
    far = noise * (0.6 / TILE)
    affinity = jnp.where(diagonal, near, far)
    return (row_weight[:, :, None] * affinity * col_weight[:, None, :]).astype(jnp.float32)


def level_of(rng, extent, split, least, high):
    level = 1.0
    for axis_at, blocks in split:
        draws = jax.random.uniform(jax.random.fold_in(jax.random.fold_in(rng, 6), axis_at), (blocks,), jnp.float32, least / len(split), high / len(split))
        level = level * jnp.repeat(jnp.exp(draws), extent[axis_at] // blocks).reshape((-1,) + (1,) * (len(extent) - 1 - axis_at))
    return level


def gaussian(key, extent, deviation, reach, shards=(), held_as=jnp.bfloat16):
    factor_of = level_of(key, extent, shards, -0.22, 0.18) if shards else 1.0
    entries = jax.random.normal(key, extent, jnp.float32) * deviation * factor_of
    return jnp.minimum(jnp.maximum(entries, -reach), reach).astype(held_as)


def setup_inputs(seed: int = 0) -> dict:
    splits = jax.random.split(jax.random.key(seed), 5)
    return {
        "tiles": draw_tiles(jax.random.fold_in(splits[4], 71), 0),
        "coords": draw_coords(jax.random.fold_in(splits[4], 71), 0),
        "live": draw_live(jax.random.fold_in(splits[4], 71), 0),
        "sketch": gaussian(splits[3], (NROWS, K), 1.0, 6.0, ((0, 32),), jnp.float32),
    }


HIGHEST = lax.Precision.HIGHEST

def apply_graph(tiles, coords, live, panel, transpose):
    panel_tiles = panel.reshape(DEVICES * TPD, TILE, K)
    initial = jnp.zeros((DEVICES * TPD, TILE, K), jnp.float32)
    slot_ids = jnp.arange(CAP, dtype=jnp.int32)

    def device_step(device, summed):
        offset = (device * CAP).astype(jnp.int32)
        tile_slab = lax.dynamic_slice_in_dim(tiles, offset, CAP, 0)
        spots = lax.dynamic_slice_in_dim(coords, offset, CAP, 0)
        active = (slot_ids < live[device]).astype(jnp.float32)
        if transpose:
            fetched = panel_tiles[spots[:, 0]]
            product = jnp.einsum('sji,sjk->sik', tile_slab, fetched, precision=HIGHEST)
            placed = spots[:, 1]
        else:
            fetched = panel_tiles[spots[:, 1]]
            product = jnp.einsum('sij,sjk->sik', tile_slab, fetched, precision=HIGHEST)
            placed = spots[:, 0]
        return summed.at[placed].add(product * active[:, None, None])
    result = lax.fori_loop(0, DEVICES, device_step, initial)
    return result.reshape(DEVICES * TPD * TILE, K)

def orthonormal(image):
    gram = jnp.dot(image.T.astype(jnp.float32), image.astype(jnp.float32), precision=HIGHEST, preferred_element_type=jnp.float32)
    lower = jnp.linalg.cholesky(gram)
    return jax.scipy.linalg.solve_triangular(lower, image.T, lower=True).T

def reference(tiles, coords, live, sketch):
    panel = sketch
    for sweep in range(2):
        spread = apply_graph(tiles, coords, live, panel, True)
        image = apply_graph(tiles, coords, live, spread, False)
        panel = orthonormal(image)
    return panel * NROWS ** 0.5
```

```python
import functools

import jax
import jax.numpy as jnp
from jax import lax
from jax.experimental import pallas as pl
from jax.experimental.pallas import tpu as pltpu
from jax.sharding import PartitionSpec as P

HIGHEST = lax.Precision.HIGHEST
MESH = pl.DeviceIdType.MESH
SWEEPS = 2
SUB = 2
UNROLL = 8
PIVOTS = 4


def radices(count):
    found = []
    while count > 1:
        radix = 4 if count % 4 == 0 else next(r for r in range(2, count + 1) if count % r == 0)
        found.append(radix)
        count //= radix
    return found


def dot(a, b):
    return jnp.dot(a, b, precision=HIGHEST, preferred_element_type=jnp.float32)


def dot_nt(a, b, precision=None):
    return lax.dot_general(
        a, b, (((1,), (1,)), ((), ())), precision=precision, preferred_element_type=jnp.float32
    )


def halves(x):
    high = x.astype(jnp.bfloat16)
    low = (x - high.astype(jnp.float32)).astype(jnp.bfloat16)
    return high, low


def inverse_factor(packed, k):
    half = k // 2
    lane = lax.broadcasted_iota(jnp.int32, (half, 2 * k), 1)
    row = lax.broadcasted_iota(jnp.int32, (half, 2 * k), 0)
    one = jnp.float32(1.0)
    zero = jnp.float32(0.0)
    top = jnp.where(lane >= k, pltpu.roll(packed, k, 1), jnp.where(lane == row, one, zero))
    low = jnp.where(lane >= k, packed, jnp.where(lane == row + half, one, zero))
    m = jnp.concatenate([top, low], axis=0)
    rows = lax.broadcasted_iota(jnp.int32, (k, 2 * k), 0)
    pivots = jnp.ones((k, 2 * k), jnp.float32)
    for j in range(0, k, PIVOTS):
        cols = [
            jnp.broadcast_to(m[:, k + j + i : k + j + i + 1], (k, 2 * k)) for i in range(PIVOTS)
        ]
        lines = [m[j + i : j + i + 1, :] for i in range(PIVOTS)]
        for i in range(PIVOTS):
            pivot = cols[i][j + i : j + i + 1, :]
            pivots = jnp.where(rows == j + i, pivot, pivots)
            factor = jnp.where(rows > j + i, cols[i] * (1.0 / pivot), 0.0)
            for n in range(i + 1, PIVOTS):
                lines[n] = lines[n] - factor[j + n : j + n + 1, :] * lines[i]
                cols[n] = cols[n] - factor * cols[i][j + n : j + n + 1, :]
            m = m - factor * lines[i]
    return (m * lax.rsqrt(pivots))[:, :k]


def kernel(
    n_rows, n_grp, total_rows, meta, tiles, sketch, out,
    t2, run, part, rcv1, rcv2, rcv3, spr, img, gbuf, grest, send_sem, recv_sem,
):
    cap, edge, _ = tiles.shape
    tpd, k, _ = img.shape
    half = k // 2
    n_hi = n_grp // 2
    block_tiles = n_grp * tpd
    width = tpd // SUB
    row = lax.axis_index("rows")
    grp = lax.axis_index("grp")
    lo = lax.rem(grp, 2)
    hi = grp // 2
    after = lax.rem(row + 1, n_rows)
    before = lax.rem(row + n_rows - 1, n_rows)
    core_peer = (row, hi * 2 + 1 - lo)

    def hi_peer(step):
        return lax.rem(hi + step, n_hi) * 2 + lo

    near_size = 2 * n_grp
    near_me = lax.rem(row, 2) * n_grp + grp

    def near_peer(step):
        at = lax.rem(near_me + step, near_size)
        return (row // 2 * 2 + at // n_grp, lax.rem(at, n_grp))

    rest = []
    stride = 2
    for radix in radices(n_rows // 2):
        digit = lax.rem(row // stride, radix)
        rest.append((radix, stride, digit))
        stride *= radix

    def rest_peer(stage, step):
        radix, stride, digit = rest[stage]
        return (row + (lax.rem(digit + step, radix) - digit) * stride, grp)

    peers = [(after, grp), (before, grp)]
    peers += [near_peer(s) for s in range(1, near_size)]
    for stage in range(len(rest)):
        peers += [rest_peer(stage, s) for s in range(1, rest[stage][0])]
    barrier = pltpu.get_barrier_semaphore()
    for peer in peers:
        pl.semaphore_signal(barrier, inc=1, device_id=peer, device_id_type=MESH)

    started = []

    def send(src, dst, peer):
        at = len(started)
        copy = pltpu.make_async_remote_copy(
            src_ref=src, dst_ref=dst, send_sem=send_sem.at[at], recv_sem=recv_sem.at[at],
            device_id=peer, device_id_type=MESH,
        )
        copy.start()
        started.append(copy)
        return copy

    def prev_of(s):
        return meta[s]

    def row_of(s):
        return meta[cap + s]

    def col_of(s):
        return meta[2 * cap + s]

    def last_of(t):
        return meta[3 * cap + t]

    run[0] = jnp.zeros((k, edge), jnp.float32)
    for t in range(tpd):
        img[t] = sketch[t * edge : (t + 1) * edge, :].T

    def spread_sweep(first):
        def step(number, carry):
            base = number * UNROLL
            products = []
            for u in range(UNROLL):
                s = base + u
                if first:
                    t_high, t_low = halves(tiles[s])
                    t2[s, 0:edge, :] = t_high
                    t2[s, edge : 2 * edge, :] = t_low
                else:
                    t_high = t2[s, 0:edge, :]
                    t_low = t2[s, edge : 2 * edge, :]
                high, low = halves(img[jnp.maximum(row_of(s), 0)])
                both = jnp.dot(
                    jnp.concatenate([high, low], axis=0), t_high,
                    preferred_element_type=jnp.float32,
                )
                cross = jnp.dot(high, t_low, preferred_element_type=jnp.float32)
                products.append(both[0:k] + (both[k : 2 * k] + cross))
            for u in range(UNROLL):
                s = base + u
                run[s + 1] = products[u] + run[prev_of(s)]
            return carry

        lax.fori_loop(0, cap // UNROLL, step, 0)

    def image_sweep(it):
        for t in range(tpd):
            img[t] = jnp.zeros((k, edge), jnp.float32)

        def step(number, carry):
            base = number * UNROLL
            sums = [None] * tpd
            for u in range(UNROLL):
                s = base + u
                high, low = halves(spr[it, col_of(s)])
                t_high = t2[s, 0:edge, :]
                t_low = t2[s, edge : 2 * edge, :]
                both = dot_nt(jnp.concatenate([high, low], axis=0), t_high)
                cross = dot_nt(high, t_low)
                product = both[0:k] + (both[k : 2 * k] + cross)
                at = row_of(s)
                for t in range(tpd):
                    term = jnp.where(at == t, jnp.float32(1.0), jnp.float32(0.0)) * product
                    sums[t] = term if sums[t] is None else sums[t] + term
            for t in range(tpd):
                img[t] = img[t] + sums[t]
            return carry

        lax.fori_loop(0, cap // UNROLL, step, 0)

    def gram_begin(it):
        total = None
        for t in range(tpd):
            tile = img[t]
            term = dot_nt(tile, jnp.concatenate([tile, tile], axis=0), HIGHEST)
            total = term if total is None else total + term
        lane = lax.broadcasted_iota(jnp.int32, (half, 2 * k), 1)
        gbuf[it, near_me] = jnp.where(lane < k, total[0:half], total[half:k])
        return [
            send(gbuf.at[it, near_me], gbuf.at[it, near_me], near_peer(s))
            for s in range(1, near_size)
        ]

    def gram_near(it, copies):
        for copy in copies:
            copy.wait_recv()
        total = gbuf[it, 0]
        for a in range(1, near_size):
            total = total + gbuf[it, a]
        return total

    def gram_rest_begin(it, stage, total):
        base = sum(r for r, _, _ in rest[:stage])
        radix, _, digit = rest[stage]
        grest[it, base + digit] = total
        return [
            send(grest.at[it, base + digit], grest.at[it, base + digit], rest_peer(stage, s))
            for s in range(1, radix)
        ]

    def gram_rest_end(it, stage, copies):
        base = sum(r for r, _, _ in rest[:stage])
        for copy in copies:
            copy.wait_recv()
        total = grest[it, base]
        for a in range(1, rest[stage][0]):
            total = total + grest[it, base + a]
        return total

    def gram_rest(it, total, copies):
        for stage in range(len(rest)):
            if copies is None:
                copies = gram_rest_begin(it, stage, total)
            total = gram_rest_end(it, stage, copies)
            copies = None
        return total

    def tiles_at(block, g, t=0):
        return block * block_tiles + g * tpd + t

    order = (0, 2, 1)

    def fill(it, block, g):
        def one(t, carry):
            at = tiles_at(block, g) + t
            part[it, at] = run[last_of(at)]
            return carry

        lax.fori_loop(0, tpd, one, 0)

    def scatter_core(it):
        copies = {}
        for block in order:
            for h in range(n_hi):
                g = h * 2 + 1 - lo
                fill(it, block, g)
                copies[block, h] = send(
                    part.at[it, pl.ds(tiles_at(block, g), tpd)],
                    rcv1.at[it, pl.ds((block * n_hi + h) * tpd, tpd)],
                    core_peer,
                )
        for block in order:
            for h in range(n_hi):
                fill(it, block, h * 2 + lo)
        return copies

    def scatter_hi(it, core_copies):
        copies = {}
        for block in order:
            for h in range(n_hi):
                core_copies[block, h].wait_recv()
            for step in range(1, n_hi):
                h = lax.rem(hi + step, n_hi)
                at = tiles_at(block, h * 2 + lo)
                from_core = (block * n_hi + h) * tpd
                for c in range(SUB):
                    mine = pl.ds(at + c * width, width)
                    part[it, mine] = part[it, mine] + rcv1[it, pl.ds(from_core + c * width, width)]
                    slot = (block * (n_hi - 1) + step - 1) * tpd + c * width
                    copies[block, step, c] = send(
                        part.at[it, mine], rcv2.at[it, pl.ds(slot, width)], (row, hi_peer(step))
                    )
        return copies

    def scatter_rows(it, hi_copies):
        copies = []
        for block in order:
            for c in range(SUB):
                mine = pl.ds(tiles_at(block, grp) + c * width, width)
                total = part[it, mine] + rcv1[
                    it, pl.ds((block * n_hi + hi) * tpd + c * width, width)
                ]
                for step in range(1, n_hi):
                    hi_copies[block, step, c].wait_recv()
                    slot = (block * (n_hi - 1) + step - 1) * tpd + c * width
                    total = total + rcv2[it, pl.ds(slot, width)]
                part[it, mine] = total
                if block == 0:
                    copies.append(
                        send(part.at[it, mine], rcv3.at[it, pl.ds(c * width, width)], (before, grp))
                    )
                if block == 2:
                    copies.append(
                        send(
                            part.at[it, mine],
                            rcv3.at[it, pl.ds(tpd + c * width, width)],
                            (after, grp),
                        )
                    )
        return copies

    def gather(it, row_copies, inverse):
        lead = []
        for c in range(SUB):
            row_copies[c].wait_recv()
            row_copies[SUB + c].wait_recv()
            for w in range(width):
                t = c * width + w
                value = part[it, tiles_at(1, grp) + t] + (rcv3[it, t] + rcv3[it, tpd + t])
                if inverse is not None:
                    value = dot(inverse, value)
                spr[it, tiles_at(1, grp) + t] = value

            def at(block, g, c=c):
                return spr.at[it, pl.ds(tiles_at(block, g) + c * width, width)]

            own = at(1, grp)
            up = send(own, at(0, grp), (after, grp))
            down = send(own, at(2, grp), (before, grp))
            across = [send(own, at(1, grp), (row, hi_peer(s))) for s in range(1, n_hi)]
            core = send(own, at(1, grp), core_peer)
            lead.append((up, down, across, core, at))
        last = []
        later = []
        for up, down, across, core, at in lead:
            last.append(core)
            for block, copy in ((0, up), (2, down)):
                copy.wait_recv()
                piece = at(block, grp)
                for s in range(1, n_hi):
                    later.append((block, s, at, send(piece, piece, (row, hi_peer(s)))))
                last.append(send(piece, piece, core_peer))
            for s in range(1, n_hi):
                across[s - 1].wait_recv()
                piece = at(1, hi_peer(n_hi - s))
                last.append(send(piece, piece, core_peer))
        for block, s, at, copy in later:
            copy.wait_recv()
            piece = at(block, hi_peer(n_hi - s))
            last.append(send(piece, piece, core_peer))
        for copy in last:
            copy.wait_recv()

    inverse = None
    near = None
    for it in range(SWEEPS):
        spread_sweep(it == 0)
        if it == 0:
            pl.semaphore_wait(barrier, len(peers))
        core_copies = scatter_core(it)
        far = None
        if near is not None:
            total = gram_near(it - 1, near)
            if rest:
                far = gram_rest_begin(it - 1, 0, total)
        hi_copies = scatter_hi(it, core_copies)
        row_copies = scatter_rows(it, hi_copies)
        if near is not None:
            inverse = inverse_factor(gram_rest(it - 1, total, far), k)
        gather(it, row_copies, inverse)
        image_sweep(it)
        near = gram_begin(it)
    total = gram_rest(SWEEPS - 1, gram_near(SWEEPS - 1, near), None)
    inverse = inverse_factor(total, k) * jnp.float32(total_rows**0.5)
    for t in range(tpd):
        out[:, t * edge : (t + 1) * edge] = dot(inverse, img[t])
    for copy in started:
        copy.wait_send()


def copies_of(n_rows, n_grp):
    n_hi = n_grp // 2
    scatter = 3 * n_hi + 3 * (n_hi - 1) * SUB + 2 * SUB
    gather = SUB * (2 + (n_hi - 1) + 1 + 2 * n_hi + 3 * (n_hi - 1))
    gram = 2 * n_grp - 1 + sum(r - 1 for r in radices(n_rows // 2))
    return SWEEPS * (scatter + gather + gram)


def local(tiles, coords, live, sketch):
    n_grp = lax.axis_size("grp")
    n_rows = lax.axis_size("rows")
    row = lax.axis_index("rows")
    grp = lax.axis_index("grp")
    cap, edge, _ = tiles.shape
    k = sketch.shape[1]
    tpd = sketch.shape[0] // edge
    block_tiles = n_grp * tpd
    targets = 3 * block_tiles
    slots = jnp.arange(cap, dtype=jnp.int32)
    used = slots < live[0]
    row_pos = coords[:, 0] - (row * block_tiles + grp * tpd)
    col_tiles = coords[:, 1]
    col_pos = (
        (col_tiles // block_tiles - row + 1 + n_rows) % n_rows * block_tiles
        + col_tiles % block_tiles
    )
    wanted = jnp.concatenate([col_pos, jnp.arange(targets, dtype=jnp.int32)])
    until = jnp.concatenate([slots, jnp.full((targets,), cap, jnp.int32)])
    same = (wanted[:, None] == col_pos[None, :]) & used[None, :] & (slots[None, :] < until[:, None])
    link = jnp.max(jnp.where(same, slots[None, :] + 1, 0), axis=1)
    meta = jnp.concatenate(
        [
            link[:cap],
            jnp.where(used, row_pos, -1),
            jnp.clip(col_pos, 0, targets - 1),
            link[cap:],
        ]
    )
    n_hi = n_grp // 2
    n_copies = copies_of(n_rows, n_grp)
    f32 = jnp.float32
    vmem = pl.BlockSpec(memory_space=pltpu.VMEM)
    basis = pl.pallas_call(
        functools.partial(kernel, n_rows, n_grp, n_rows * n_grp * sketch.shape[0]),
        out_shape=jax.ShapeDtypeStruct((k, tpd * edge), f32),
        in_specs=[pl.BlockSpec(memory_space=pltpu.SMEM), vmem, vmem],
        out_specs=vmem,
        scratch_shapes=[
            pltpu.VMEM((cap, 2 * edge, edge), jnp.bfloat16),
            pltpu.VMEM((cap + 1, k, edge), f32),
            pltpu.VMEM((SWEEPS, targets, k, edge), f32),
            pltpu.VMEM((SWEEPS, 3 * n_hi * tpd, k, edge), f32),
            pltpu.VMEM((SWEEPS, 3 * max(n_hi - 1, 1) * tpd, k, edge), f32),
            pltpu.VMEM((SWEEPS, 2 * tpd, k, edge), f32),
            pltpu.VMEM((SWEEPS, targets, k, edge), f32),
            pltpu.VMEM((tpd, k, edge), f32),
            pltpu.VMEM((SWEEPS, 2 * n_grp, k // 2, 2 * k), f32),
            pltpu.VMEM((SWEEPS, max(sum(radices(n_rows // 2)), 1), k // 2, 2 * k), f32),
            pltpu.SemaphoreType.DMA((n_copies,)),
            pltpu.SemaphoreType.DMA((n_copies,)),
        ],
        compiler_params=pltpu.CompilerParams(
            collective_id=0, has_side_effects=True, vmem_limit_bytes=48 * 1024 * 1024
        ),
    )(meta, tiles, sketch)
    return basis.T


def solution(mesh):
    return jax.shard_map(
        local,
        mesh=mesh,
        in_specs=(
            P(("rows", "grp"), None, None),
            P(("rows", "grp"), None),
            P(("rows", "grp")),
            P(("rows", "grp"), None),
        ),
        out_specs=P(("rows", "grp"), None),
        check_vma=False,
    )
```

```python
import functools

import jax
import jax.numpy as jnp
from jax import lax
from jax.experimental import pallas as pl
from jax.experimental.pallas import tpu as pltpu
from jax.sharding import PartitionSpec as P

HIGHEST = lax.Precision.HIGHEST
MESH = pl.DeviceIdType.MESH
SWEEPS = 2
SUB = 4
UNROLL = 8
PIVOTS = 4


def radices(count):
    found = []
    while count > 1:
        radix = 4 if count % 4 == 0 else next(r for r in range(2, count + 1) if count % r == 0)
        found.append(radix)
        count //= radix
    return found


def dot(a, b):
    return jnp.dot(a, b, precision=HIGHEST, preferred_element_type=jnp.float32)


def dot_nt(a, b, precision=None):
    return lax.dot_general(
        a, b, (((1,), (1,)), ((), ())), precision=precision, preferred_element_type=jnp.float32
    )


def halves(x):
    high = x.astype(jnp.bfloat16)
    low = (x - high.astype(jnp.float32)).astype(jnp.bfloat16)
    return high, low


def augmented(packed, k):
    half = k // 2
    lane = lax.broadcasted_iota(jnp.int32, (half, 2 * k), 1)
    row = lax.broadcasted_iota(jnp.int32, (half, 2 * k), 0)
    one = jnp.float32(1.0)
    zero = jnp.float32(0.0)
    top = jnp.where(lane >= k, pltpu.roll(packed, k, 1), jnp.where(lane == row, one, zero))
    low = jnp.where(lane >= k, packed, jnp.where(lane == row + half, one, zero))
    return jnp.concatenate([top, low], axis=0), jnp.ones((k, 2 * k), jnp.float32)


def eliminate(state, k, columns):
    m, pivots = state
    rows = lax.broadcasted_iota(jnp.int32, (k, 2 * k), 0)
    for j in columns:
        cols = [
            jnp.broadcast_to(m[:, k + j + i : k + j + i + 1], (k, 2 * k)) for i in range(PIVOTS)
        ]
        lines = [m[j + i : j + i + 1, :] for i in range(PIVOTS)]
        for i in range(PIVOTS):
            pivot = cols[i][j + i : j + i + 1, :]
            pivots = jnp.where(rows == j + i, pivot, pivots)
            factor = jnp.where(rows > j + i, cols[i] * (1.0 / pivot), 0.0)
            for n in range(i + 1, PIVOTS):
                lines[n] = lines[n] - factor[j + n : j + n + 1, :] * lines[i]
                cols[n] = cols[n] - factor * cols[i][j + n : j + n + 1, :]
            m = m - factor * lines[i]
    return m, pivots


def inverse_of(state, k):
    m, pivots = state
    return (m * lax.rsqrt(pivots))[:, :k]


def kernel(
    n_rows, n_grp, total_rows, meta, stored, sketch, out,
    tiles, t2, run, part, rcv1, rcv2, rcv3, spr, img, gbuf, grest, load_sem, send_sem, recv_sem,
):
    cap, edge, _ = tiles.shape
    tpd, k, _ = img.shape
    half = k // 2
    n_hi = n_grp // 2
    block_tiles = n_grp * tpd
    width = tpd // SUB
    row = lax.axis_index("rows")
    grp = lax.axis_index("grp")
    lo = lax.rem(grp, 2)
    hi = grp // 2
    after = lax.rem(row + 1, n_rows)
    before = lax.rem(row + n_rows - 1, n_rows)
    core_peer = (row, hi * 2 + 1 - lo)

    def hi_peer(step):
        return lax.rem(hi + step, n_hi) * 2 + lo

    near_size = 2 * n_grp
    near_me = lax.rem(row, 2) * n_grp + grp

    def near_peer(step):
        at = lax.rem(near_me + step, near_size)
        return (row // 2 * 2 + at // n_grp, lax.rem(at, n_grp))

    rest = []
    stride = 2
    for radix in radices(n_rows // 2):
        digit = lax.rem(row // stride, radix)
        rest.append((radix, stride, digit))
        stride *= radix

    def rest_peer(stage, step):
        radix, stride, digit = rest[stage]
        return (row + (lax.rem(digit + step, radix) - digit) * stride, grp)

    def load(number):
        some = pl.ds(number * UNROLL, UNROLL)
        return pltpu.make_async_copy(stored.at[some], tiles.at[some], load_sem.at[number])

    for number in range(cap // UNROLL):
        load(number).start()

    peers = [(after, grp), (before, grp)]
    peers += [near_peer(s) for s in range(1, near_size)]
    for stage in range(len(rest)):
        peers += [rest_peer(stage, s) for s in range(1, rest[stage][0])]
    barrier = pltpu.get_barrier_semaphore()
    for peer in peers:
        pl.semaphore_signal(barrier, inc=1, device_id=peer, device_id_type=MESH)

    started = []

    def send(src, dst, peer):
        at = len(started)
        copy = pltpu.make_async_remote_copy(
            src_ref=src, dst_ref=dst, send_sem=send_sem.at[at], recv_sem=recv_sem.at[at],
            device_id=peer, device_id_type=MESH,
        )
        copy.start()
        started.append(copy)
        return copy

    def prev_of(s):
        return meta[s]

    def row_of(s):
        return meta[cap + s]

    def col_of(s):
        return meta[2 * cap + s]

    def last_of(t):
        return meta[3 * cap + t]

    run[0] = jnp.zeros((k, edge), jnp.float32)
    for t in range(tpd):
        img[t] = sketch[:, t * edge : (t + 1) * edge]

    def spread_sweep(first):
        def step(number, carry):
            base = number * UNROLL
            products = []
            if first:
                load(number).wait()
            for u in range(UNROLL):
                s = base + u
                if first:
                    t_high, t_low = halves(tiles[s])
                    t2[s, 0:edge, :] = t_high
                    t2[s, edge : 2 * edge, :] = t_low
                else:
                    t_high = t2[s, 0:edge, :]
                    t_low = t2[s, edge : 2 * edge, :]
                high, low = halves(img[jnp.maximum(row_of(s), 0)])
                both = jnp.dot(
                    jnp.concatenate([high, low], axis=0), t_high,
                    preferred_element_type=jnp.float32,
                )
                cross = jnp.dot(high, t_low, preferred_element_type=jnp.float32)
                products.append(both[0:k] + (both[k : 2 * k] + cross))
            for u in range(UNROLL):
                s = base + u
                run[s + 1] = products[u] + run[prev_of(s)]
            return carry

        lax.fori_loop(0, cap // UNROLL, step, 0)

    def image_sweep(it):
        for t in range(tpd):
            img[t] = jnp.zeros((k, edge), jnp.float32)

        def step(number, carry):
            base = number * UNROLL
            sums = [None] * tpd
            for u in range(UNROLL):
                s = base + u
                high, low = halves(spr[it, col_of(s)])
                t_high = t2[s, 0:edge, :]
                t_low = t2[s, edge : 2 * edge, :]
                both = dot_nt(jnp.concatenate([high, low], axis=0), t_high)
                cross = dot_nt(high, t_low)
                product = both[0:k] + (both[k : 2 * k] + cross)
                at = row_of(s)
                for t in range(tpd):
                    term = jnp.where(at == t, jnp.float32(1.0), jnp.float32(0.0)) * product
                    sums[t] = term if sums[t] is None else sums[t] + term
            for t in range(tpd):
                img[t] = img[t] + sums[t]
            return carry

        lax.fori_loop(0, cap // UNROLL, step, 0)

    def gram_begin(it):
        total = None
        for t in range(tpd):
            tile = img[t]
            term = dot_nt(tile, jnp.concatenate([tile, tile], axis=0), HIGHEST)
            total = term if total is None else total + term
        lane = lax.broadcasted_iota(jnp.int32, (half, 2 * k), 1)
        gbuf[it, near_me] = jnp.where(lane < k, total[0:half], total[half:k])
        return [
            send(gbuf.at[it, near_me], gbuf.at[it, near_me], near_peer(s))
            for s in range(1, near_size)
        ]

    def gram_near(it, copies):
        for copy in copies:
            copy.wait_recv()
        total = gbuf[it, 0]
        for a in range(1, near_size):
            total = total + gbuf[it, a]
        return total

    def gram_rest_begin(it, stage, total):
        base = sum(r for r, _, _ in rest[:stage])
        radix, _, digit = rest[stage]
        grest[it, base + digit] = total
        return [
            send(grest.at[it, base + digit], grest.at[it, base + digit], rest_peer(stage, s))
            for s in range(1, radix)
        ]

    def gram_rest_end(it, stage, copies):
        base = sum(r for r, _, _ in rest[:stage])
        for copy in copies:
            copy.wait_recv()
        total = grest[it, base]
        for a in range(1, rest[stage][0]):
            total = total + grest[it, base + a]
        return total

    def gram_rest(it, total, copies):
        for stage in range(len(rest)):
            if copies is None:
                copies = gram_rest_begin(it, stage, total)
            total = gram_rest_end(it, stage, copies)
            copies = None
        return total

    def tiles_at(block, g, t=0):
        return block * block_tiles + g * tpd + t

    order = (0, 2, 1)

    def fill(it, block, g):
        def one(t, carry):
            at = tiles_at(block, g) + t
            part[it, at] = run[last_of(at)]
            return carry

        lax.fori_loop(0, tpd, one, 0)

    def scatter_core(it):
        copies = {}
        for block in order:
            for h in range(n_hi):
                g = h * 2 + 1 - lo
                fill(it, block, g)
                copies[block, h] = send(
                    part.at[it, pl.ds(tiles_at(block, g), tpd)],
                    rcv1.at[it, pl.ds((block * n_hi + h) * tpd, tpd)],
                    core_peer,
                )
        for block in order:
            for h in range(n_hi):
                fill(it, block, h * 2 + lo)
        return copies

    def scatter_hi(it, core_copies):
        copies = {}
        for block in order:
            for h in range(n_hi):
                core_copies[block, h].wait_recv()
            for step in range(1, n_hi):
                h = lax.rem(hi + step, n_hi)
                at = tiles_at(block, h * 2 + lo)
                from_core = (block * n_hi + h) * tpd
                for c in range(SUB):
                    mine = pl.ds(at + c * width, width)
                    part[it, mine] = part[it, mine] + rcv1[it, pl.ds(from_core + c * width, width)]
                    slot = (block * (n_hi - 1) + step - 1) * tpd + c * width
                    copies[block, step, c] = send(
                        part.at[it, mine], rcv2.at[it, pl.ds(slot, width)], (row, hi_peer(step))
                    )
        return copies

    def scatter_rows(it, hi_copies, blocks):
        copies = []
        for block in blocks:
            for c in range(SUB):
                mine = pl.ds(tiles_at(block, grp) + c * width, width)
                total = part[it, mine] + rcv1[
                    it, pl.ds((block * n_hi + hi) * tpd + c * width, width)
                ]
                for step in range(1, n_hi):
                    hi_copies[block, step, c].wait_recv()
                    slot = (block * (n_hi - 1) + step - 1) * tpd + c * width
                    total = total + rcv2[it, pl.ds(slot, width)]
                part[it, mine] = total
                if block == 0:
                    copies.append(
                        send(part.at[it, mine], rcv3.at[it, pl.ds(c * width, width)], (before, grp))
                    )
                if block == 2:
                    copies.append(
                        send(
                            part.at[it, mine],
                            rcv3.at[it, pl.ds(tpd + c * width, width)],
                            (after, grp),
                        )
                    )
        return copies

    def gather(it, row_copies, inverse):
        lead = []
        for c in range(SUB):
            row_copies[c].wait_recv()
            row_copies[SUB + c].wait_recv()
            for w in range(width):
                t = c * width + w
                value = part[it, tiles_at(1, grp) + t] + (rcv3[it, t] + rcv3[it, tpd + t])
                if inverse is not None:
                    value = dot(inverse, value)
                spr[it, tiles_at(1, grp) + t] = value

            def at(block, g, c=c):
                return spr.at[it, pl.ds(tiles_at(block, g) + c * width, width)]

            own = at(1, grp)
            up = send(own, at(0, grp), (after, grp))
            down = send(own, at(2, grp), (before, grp))
            across = [send(own, at(1, grp), (row, hi_peer(s))) for s in range(1, n_hi)]
            core = send(own, at(1, grp), core_peer)
            lead.append((up, down, across, core, at))
        last = []
        later = []
        for up, down, across, core, at in lead:
            last.append(core)
            for block, copy in ((0, up), (2, down)):
                copy.wait_recv()
                piece = at(block, grp)
                for s in range(1, n_hi):
                    later.append((block, s, at, send(piece, piece, (row, hi_peer(s)))))
                last.append(send(piece, piece, core_peer))
            for s in range(1, n_hi):
                across[s - 1].wait_recv()
                piece = at(1, hi_peer(n_hi - s))
                last.append(send(piece, piece, core_peer))
        for block, s, at, copy in later:
            copy.wait_recv()
            piece = at(block, hi_peer(n_hi - s))
            last.append(send(piece, piece, core_peer))
        for copy in last:
            copy.wait_recv()

    inverse = None
    near = None
    for it in range(SWEEPS):
        spread_sweep(it == 0)
        if it == 0:
            pl.semaphore_wait(barrier, len(peers))
        core_copies = scatter_core(it)
        far = None
        if near is not None:
            total = gram_near(it - 1, near)
            if rest:
                far = gram_rest_begin(it - 1, 0, total)
        hi_copies = scatter_hi(it, core_copies)
        if near is not None:
            state = augmented(gram_rest(it - 1, total, far), k)
            state = eliminate(state, k, range(0, k // 2, PIVOTS))
        row_copies = scatter_rows(it, hi_copies, order[:2])
        if near is not None:
            inverse = inverse_of(eliminate(state, k, range(k // 2, k, PIVOTS)), k)
        scatter_rows(it, hi_copies, order[2:])
        gather(it, row_copies, inverse)
        image_sweep(it)
        near = gram_begin(it)
    total = gram_rest(SWEEPS - 1, gram_near(SWEEPS - 1, near), None)
    state = eliminate(augmented(total, k), k, range(0, k, PIVOTS))
    inverse = inverse_of(state, k) * jnp.float32(total_rows**0.5)
    for t in range(tpd):
        out[:, t * edge : (t + 1) * edge] = dot(inverse, img[t])
    for copy in started:
        copy.wait_send()


def copies_of(n_rows, n_grp):
    n_hi = n_grp // 2
    scatter = 3 * n_hi + 3 * (n_hi - 1) * SUB + 2 * SUB
    gather = SUB * (2 + (n_hi - 1) + 1 + 2 * n_hi + 3 * (n_hi - 1))
    gram = 2 * n_grp - 1 + sum(r - 1 for r in radices(n_rows // 2))
    return SWEEPS * (scatter + gather + gram)


def local(tiles, coords, live, sketch):
    n_grp = lax.axis_size("grp")
    n_rows = lax.axis_size("rows")
    row = lax.axis_index("rows")
    grp = lax.axis_index("grp")
    cap, edge, _ = tiles.shape
    k = sketch.shape[1]
    tpd = sketch.shape[0] // edge
    block_tiles = n_grp * tpd
    targets = 3 * block_tiles
    slots = jnp.arange(cap, dtype=jnp.int32)
    used = slots < live[0]
    row_pos = coords[:, 0] - (row * block_tiles + grp * tpd)
    col_tiles = coords[:, 1]
    col_pos = (
        (col_tiles // block_tiles - row + 1 + n_rows) % n_rows * block_tiles
        + col_tiles % block_tiles
    )
    wanted = jnp.concatenate([col_pos, jnp.arange(targets, dtype=jnp.int32)])
    until = jnp.concatenate([slots, jnp.full((targets,), cap, jnp.int32)])
    same = (wanted[:, None] == col_pos[None, :]) & used[None, :] & (slots[None, :] < until[:, None])
    link = jnp.max(jnp.where(same, slots[None, :] + 1, 0), axis=1)
    meta = jnp.concatenate(
        [
            link[:cap],
            jnp.where(used, row_pos, -1),
            jnp.clip(col_pos, 0, targets - 1),
            link[cap:],
        ]
    )
    n_hi = n_grp // 2
    n_copies = copies_of(n_rows, n_grp)
    f32 = jnp.float32
    vmem = pl.BlockSpec(memory_space=pltpu.VMEM)
    basis = pl.pallas_call(
        functools.partial(kernel, n_rows, n_grp, n_rows * n_grp * sketch.shape[0]),
        out_shape=jax.ShapeDtypeStruct((k, tpd * edge), f32),
        in_specs=[
            pl.BlockSpec(memory_space=pltpu.SMEM), pl.BlockSpec(memory_space=pltpu.HBM), vmem,
        ],
        out_specs=vmem,
        scratch_shapes=[
            pltpu.VMEM((cap, edge, edge), f32),
            pltpu.VMEM((cap, 2 * edge, edge), jnp.bfloat16),
            pltpu.VMEM((cap + 1, k, edge), f32),
            pltpu.VMEM((SWEEPS, targets, k, edge), f32),
            pltpu.VMEM((SWEEPS, 3 * n_hi * tpd, k, edge), f32),
            pltpu.VMEM((SWEEPS, 3 * max(n_hi - 1, 1) * tpd, k, edge), f32),
            pltpu.VMEM((SWEEPS, 2 * tpd, k, edge), f32),
            pltpu.VMEM((SWEEPS, targets, k, edge), f32),
            pltpu.VMEM((tpd, k, edge), f32),
            pltpu.VMEM((SWEEPS, 2 * n_grp, k // 2, 2 * k), f32),
            pltpu.VMEM((SWEEPS, max(sum(radices(n_rows // 2)), 1), k // 2, 2 * k), f32),
            pltpu.SemaphoreType.DMA((cap // UNROLL,)),
            pltpu.SemaphoreType.DMA((n_copies,)),
            pltpu.SemaphoreType.DMA((n_copies,)),
        ],
        compiler_params=pltpu.CompilerParams(
            collective_id=0, has_side_effects=True, vmem_limit_bytes=48 * 1024 * 1024
        ),
    )(meta, tiles, sketch.T)
    return basis.T


def solution(mesh):
    return jax.shard_map(
        local,
        mesh=mesh,
        in_specs=(
            P(("rows", "grp"), None, None),
            P(("rows", "grp"), None),
            P(("rows", "grp")),
            P(("rows", "grp"), None),
        ),
        out_specs=P(("rows", "grp"), None),
        check_vma=False,
    )
```

```python
import functools

import jax
import jax.numpy as jnp
from jax import lax
from jax.experimental import pallas as pl
from jax.experimental.pallas import tpu as pltpu
from jax.sharding import PartitionSpec as P

HIGHEST = lax.Precision.HIGHEST
MESH = pl.DeviceIdType.MESH
SWEEPS = 2
SUB = 4
UNROLL = 8
PIVOTS = 4


def radices(count):
    found = []
    while count > 1:
        radix = 4 if count % 4 == 0 else next(r for r in range(2, count + 1) if count % r == 0)
        found.append(radix)
        count //= radix
    return found


def dot(a, b):
    return jnp.dot(a, b, precision=HIGHEST, preferred_element_type=jnp.float32)


def dot_nt(a, b, precision=None):
    return lax.dot_general(
        a, b, (((1,), (1,)), ((), ())), precision=precision, preferred_element_type=jnp.float32
    )


def halves(x):
    high = x.astype(jnp.bfloat16)
    low = (x - high.astype(jnp.float32)).astype(jnp.bfloat16)
    return high, low


def quarters(x):
    rows, columns = x.shape[0] // 2, x.shape[1] // 2
    return x[:rows, :columns] + (
        (x[rows:, :columns] + x[:rows, columns:]) + x[rows:, columns:]
    )


def augmented(packed, k):
    half = k // 2
    lane = lax.broadcasted_iota(jnp.int32, (half, 2 * k), 1)
    row = lax.broadcasted_iota(jnp.int32, (half, 2 * k), 0)
    one = jnp.float32(1.0)
    zero = jnp.float32(0.0)
    top = jnp.where(lane >= k, pltpu.roll(packed, k, 1), jnp.where(lane == row, one, zero))
    low = jnp.where(lane >= k, packed, jnp.where(lane == row + half, one, zero))
    return jnp.concatenate([top, low], axis=0), jnp.ones((k, 2 * k), jnp.float32)


def eliminate(state, k, columns):
    m, pivots = state
    rows = lax.broadcasted_iota(jnp.int32, (k, 2 * k), 0)
    for j in columns:
        cols = [
            jnp.broadcast_to(m[:, k + j + i : k + j + i + 1], (k, 2 * k)) for i in range(PIVOTS)
        ]
        lines = [m[j + i : j + i + 1, :] for i in range(PIVOTS)]
        for i in range(PIVOTS):
            pivot = cols[i][j + i : j + i + 1, :]
            pivots = jnp.where(rows == j + i, pivot, pivots)
            factor = jnp.where(rows > j + i, cols[i] * (1.0 / pivot), 0.0)
            for n in range(i + 1, PIVOTS):
                lines[n] = lines[n] - factor[j + n : j + n + 1, :] * lines[i]
                cols[n] = cols[n] - factor * cols[i][j + n : j + n + 1, :]
            m = m - factor * lines[i]
    return m, pivots


def inverse_of(state, k):
    m, pivots = state
    return (m * lax.rsqrt(pivots))[:, :k]


def kernel(
    n_rows, n_grp, total_rows, meta, stored, sketch, out,
    tiles, t2, t3, run, part, rcv1, rcv2, rcv3, spr, img, gbuf, grest, load_sem, send_sem, recv_sem,
):
    cap, edge, _ = tiles.shape
    tpd, k, _ = img.shape
    half = k // 2
    n_hi = n_grp // 2
    block_tiles = n_grp * tpd
    width = tpd // SUB
    row = lax.axis_index("rows")
    grp = lax.axis_index("grp")
    lo = lax.rem(grp, 2)
    hi = grp // 2
    after = lax.rem(row + 1, n_rows)
    before = lax.rem(row + n_rows - 1, n_rows)
    core_peer = (row, hi * 2 + 1 - lo)

    def hi_peer(step):
        return lax.rem(hi + step, n_hi) * 2 + lo

    near_size = 2 * n_grp
    near_me = lax.rem(row, 2) * n_grp + grp

    def near_peer(step):
        at = lax.rem(near_me + step, near_size)
        return (row // 2 * 2 + at // n_grp, lax.rem(at, n_grp))

    rest = []
    stride = 2
    for radix in radices(n_rows // 2):
        digit = lax.rem(row // stride, radix)
        rest.append((radix, stride, digit))
        stride *= radix

    def rest_peer(stage, step):
        radix, stride, digit = rest[stage]
        return (row + (lax.rem(digit + step, radix) - digit) * stride, grp)

    def load(number):
        some = pl.ds(number * UNROLL, UNROLL)
        return pltpu.make_async_copy(stored.at[some], tiles.at[some], load_sem.at[number])

    for number in range(cap // UNROLL):
        load(number).start()

    peers = [(after, grp), (before, grp)]
    peers += [near_peer(s) for s in range(1, near_size)]
    for stage in range(len(rest)):
        peers += [rest_peer(stage, s) for s in range(1, rest[stage][0])]
    barrier = pltpu.get_barrier_semaphore()
    for peer in peers:
        pl.semaphore_signal(barrier, inc=1, device_id=peer, device_id_type=MESH)

    started = []

    def send(src, dst, peer):
        at = len(started)
        copy = pltpu.make_async_remote_copy(
            src_ref=src, dst_ref=dst, send_sem=send_sem.at[at], recv_sem=recv_sem.at[at],
            device_id=peer, device_id_type=MESH,
        )
        copy.start()
        started.append(copy)
        return copy

    def prev_of(s):
        return meta[s]

    def row_of(s):
        return meta[cap + s]

    def col_of(s):
        return meta[2 * cap + s]

    def last_of(t):
        return meta[3 * cap + t]

    run[0] = jnp.zeros((k, edge), jnp.float32)
    for t in range(tpd):
        img[t] = sketch[:, t * edge : (t + 1) * edge]

    def spread_sweep(first):
        def step(number, carry):
            base = number * UNROLL
            products = []
            if first:
                load(number).wait()
            for u in range(UNROLL):
                s = base + u
                if first:
                    t_high, t_low = halves(tiles[s])
                    t2[s, 0:edge, :] = t_high
                    t2[s, edge : 2 * edge, :] = t_low
                    wide = jnp.concatenate([t_high, t_low], axis=1)
                    t3[s] = wide
                else:
                    wide = t3[s]
                high, low = halves(img[jnp.maximum(row_of(s), 0)])
                products.append(
                    quarters(
                        jnp.dot(
                            jnp.concatenate([high, low], axis=0), wide,
                            preferred_element_type=jnp.float32,
                        )
                    )
                )
            for u in range(UNROLL):
                s = base + u
                run[s + 1] = products[u] + run[prev_of(s)]
            return carry

        lax.fori_loop(0, cap // UNROLL, step, 0)

    def image_sweep(it):
        for t in range(tpd):
            img[t] = jnp.zeros((k, edge), jnp.float32)

        def step(number, carry):
            base = number * UNROLL
            sums = [None] * tpd
            for u in range(UNROLL):
                s = base + u
                high, low = halves(spr[it, col_of(s)])
                product = quarters(dot_nt(jnp.concatenate([high, low], axis=0), t2[s]))
                at = row_of(s)
                for t in range(tpd):
                    term = jnp.where(at == t, jnp.float32(1.0), jnp.float32(0.0)) * product
                    sums[t] = term if sums[t] is None else sums[t] + term
            for t in range(tpd):
                img[t] = img[t] + sums[t]
            return carry

        lax.fori_loop(0, cap // UNROLL, step, 0)

    def gram_begin(it):
        total = None
        for t in range(tpd):
            tile = img[t]
            term = dot_nt(tile, jnp.concatenate([tile, tile], axis=0), HIGHEST)
            total = term if total is None else total + term
        lane = lax.broadcasted_iota(jnp.int32, (half, 2 * k), 1)
        gbuf[it, near_me] = jnp.where(lane < k, total[0:half], total[half:k])
        return [
            send(gbuf.at[it, near_me], gbuf.at[it, near_me], near_peer(s))
            for s in range(1, near_size)
        ]

    def gram_near(it, copies):
        for copy in copies:
            copy.wait_recv()
        total = gbuf[it, 0]
        for a in range(1, near_size):
            total = total + gbuf[it, a]
        return total

    def gram_rest_begin(it, stage, total):
        base = sum(r for r, _, _ in rest[:stage])
        radix, _, digit = rest[stage]
        grest[it, base + digit] = total
        return [
            send(grest.at[it, base + digit], grest.at[it, base + digit], rest_peer(stage, s))
            for s in range(1, radix)
        ]

    def gram_rest_end(it, stage, copies):
        base = sum(r for r, _, _ in rest[:stage])
        for copy in copies:
            copy.wait_recv()
        total = grest[it, base]
        for a in range(1, rest[stage][0]):
            total = total + grest[it, base + a]
        return total

    def gram_rest(it, total, copies):
        for stage in range(len(rest)):
            if copies is None:
                copies = gram_rest_begin(it, stage, total)
            total = gram_rest_end(it, stage, copies)
            copies = None
        return total

    def tiles_at(block, g, t=0):
        return block * block_tiles + g * tpd + t

    order = (0, 2, 1)

    def fill(it, block, g):
        def one(t, carry):
            at = tiles_at(block, g) + t
            part[it, at] = run[last_of(at)]
            return carry

        lax.fori_loop(0, tpd, one, 0)

    def scatter_core(it):
        copies = {}
        for block in order:
            for h in range(n_hi):
                g = h * 2 + 1 - lo
                fill(it, block, g)
                copies[block, h] = send(
                    part.at[it, pl.ds(tiles_at(block, g), tpd)],
                    rcv1.at[it, pl.ds((block * n_hi + h) * tpd, tpd)],
                    core_peer,
                )
        for block in order:
            for h in range(n_hi):
                fill(it, block, h * 2 + lo)
        return copies

    def scatter_hi(it, core_copies):
        copies = {}
        for block in order:
            for h in range(n_hi):
                core_copies[block, h].wait_recv()
            for step in range(1, n_hi):
                h = lax.rem(hi + step, n_hi)
                at = tiles_at(block, h * 2 + lo)
                from_core = (block * n_hi + h) * tpd
                for c in range(SUB):
                    mine = pl.ds(at + c * width, width)
                    part[it, mine] = part[it, mine] + rcv1[it, pl.ds(from_core + c * width, width)]
                    slot = (block * (n_hi - 1) + step - 1) * tpd + c * width
                    copies[block, step, c] = send(
                        part.at[it, mine], rcv2.at[it, pl.ds(slot, width)], (row, hi_peer(step))
                    )
        return copies

    def scatter_rows(it, hi_copies, blocks):
        copies = []
        for block in blocks:
            for c in range(SUB):
                mine = pl.ds(tiles_at(block, grp) + c * width, width)
                total = part[it, mine] + rcv1[
                    it, pl.ds((block * n_hi + hi) * tpd + c * width, width)
                ]
                for step in range(1, n_hi):
                    hi_copies[block, step, c].wait_recv()
                    slot = (block * (n_hi - 1) + step - 1) * tpd + c * width
                    total = total + rcv2[it, pl.ds(slot, width)]
                part[it, mine] = total
                if block == 0:
                    copies.append(
                        send(part.at[it, mine], rcv3.at[it, pl.ds(c * width, width)], (before, grp))
                    )
                if block == 2:
                    copies.append(
                        send(
                            part.at[it, mine],
                            rcv3.at[it, pl.ds(tpd + c * width, width)],
                            (after, grp),
                        )
                    )
        return copies

    def gather(it, row_copies, inverse):
        lead = []
        for c in range(SUB):
            row_copies[c].wait_recv()
            row_copies[SUB + c].wait_recv()
            for w in range(width):
                t = c * width + w
                value = part[it, tiles_at(1, grp) + t] + (rcv3[it, t] + rcv3[it, tpd + t])
                if inverse is not None:
                    value = dot(inverse, value)
                spr[it, tiles_at(1, grp) + t] = value

            def at(block, g, c=c):
                return spr.at[it, pl.ds(tiles_at(block, g) + c * width, width)]

            own = at(1, grp)
            up = send(own, at(0, grp), (after, grp))
            down = send(own, at(2, grp), (before, grp))
            across = [send(own, at(1, grp), (row, hi_peer(s))) for s in range(1, n_hi)]
            core = send(own, at(1, grp), core_peer)
            lead.append((up, down, across, core, at))
        last = []
        later = []
        for up, down, across, core, at in lead:
            last.append(core)
            for block, copy in ((0, up), (2, down)):
                copy.wait_recv()
                piece = at(block, grp)
                for s in range(1, n_hi):
                    later.append((block, s, at, send(piece, piece, (row, hi_peer(s)))))
                last.append(send(piece, piece, core_peer))
            for s in range(1, n_hi):
                across[s - 1].wait_recv()
                piece = at(1, hi_peer(n_hi - s))
                last.append(send(piece, piece, core_peer))
        for block, s, at, copy in later:
            copy.wait_recv()
            piece = at(block, hi_peer(n_hi - s))
            last.append(send(piece, piece, core_peer))
        for copy in last:
            copy.wait_recv()

    inverse = None
    near = None
    for it in range(SWEEPS):
        spread_sweep(it == 0)
        if it == 0:
            pl.semaphore_wait(barrier, len(peers))
        core_copies = scatter_core(it)
        far = None
        if near is not None:
            total = gram_near(it - 1, near)
            if rest:
                far = gram_rest_begin(it - 1, 0, total)
        hi_copies = scatter_hi(it, core_copies)
        if near is not None:
            state = augmented(gram_rest(it - 1, total, far), k)
            state = eliminate(state, k, range(0, k // 2, PIVOTS))
        row_copies = scatter_rows(it, hi_copies, order[:2])
        if near is not None:
            inverse = inverse_of(eliminate(state, k, range(k // 2, k, PIVOTS)), k)
        scatter_rows(it, hi_copies, order[2:])
        gather(it, row_copies, inverse)
        image_sweep(it)
        near = gram_begin(it)
    total = gram_rest(SWEEPS - 1, gram_near(SWEEPS - 1, near), None)
    state = eliminate(augmented(total, k), k, range(0, k, PIVOTS))
    inverse = inverse_of(state, k) * jnp.float32(total_rows**0.5)
    for t in range(tpd):
        out[:, t * edge : (t + 1) * edge] = dot(inverse, img[t])
    for copy in started:
        copy.wait_send()


def copies_of(n_rows, n_grp):
    n_hi = n_grp // 2
    scatter = 3 * n_hi + 3 * (n_hi - 1) * SUB + 2 * SUB
    gather = SUB * (2 + (n_hi - 1) + 1 + 2 * n_hi + 3 * (n_hi - 1))
    gram = 2 * n_grp - 1 + sum(r - 1 for r in radices(n_rows // 2))
    return SWEEPS * (scatter + gather + gram)


def local(tiles, coords, live, sketch):
    n_grp = lax.axis_size("grp")
    n_rows = lax.axis_size("rows")
    row = lax.axis_index("rows")
    grp = lax.axis_index("grp")
    cap, edge, _ = tiles.shape
    k = sketch.shape[1]
    tpd = sketch.shape[0] // edge
    block_tiles = n_grp * tpd
    targets = 3 * block_tiles
    slots = jnp.arange(cap, dtype=jnp.int32)
    used = slots < live[0]
    row_pos = coords[:, 0] - (row * block_tiles + grp * tpd)
    col_tiles = coords[:, 1]
    col_pos = (
        (col_tiles // block_tiles - row + 1 + n_rows) % n_rows * block_tiles
        + col_tiles % block_tiles
    )
    wanted = jnp.concatenate([col_pos, jnp.arange(targets, dtype=jnp.int32)])
    until = jnp.concatenate([slots, jnp.full((targets,), cap, jnp.int32)])
    same = (wanted[:, None] == col_pos[None, :]) & used[None, :] & (slots[None, :] < until[:, None])
    link = jnp.max(jnp.where(same, slots[None, :] + 1, 0), axis=1)
    meta = jnp.concatenate(
        [
            link[:cap],
            jnp.where(used, row_pos, -1),
            jnp.clip(col_pos, 0, targets - 1),
            link[cap:],
        ]
    )
    n_hi = n_grp // 2
    n_copies = copies_of(n_rows, n_grp)
    f32 = jnp.float32
    vmem = pl.BlockSpec(memory_space=pltpu.VMEM)
    basis = pl.pallas_call(
        functools.partial(kernel, n_rows, n_grp, n_rows * n_grp * sketch.shape[0]),
        out_shape=jax.ShapeDtypeStruct((k, tpd * edge), f32),
        in_specs=[
            pl.BlockSpec(memory_space=pltpu.SMEM), pl.BlockSpec(memory_space=pltpu.HBM), vmem,
        ],
        out_specs=vmem,
        scratch_shapes=[
            pltpu.VMEM((cap, edge, edge), f32),
            pltpu.VMEM((cap, 2 * edge, edge), jnp.bfloat16),
            pltpu.VMEM((cap, edge, 2 * edge), jnp.bfloat16),
            pltpu.VMEM((cap + 1, k, edge), f32),
            pltpu.VMEM((SWEEPS, targets, k, edge), f32),
            pltpu.VMEM((SWEEPS, 3 * n_hi * tpd, k, edge), f32),
            pltpu.VMEM((SWEEPS, 3 * max(n_hi - 1, 1) * tpd, k, edge), f32),
            pltpu.VMEM((SWEEPS, 2 * tpd, k, edge), f32),
            pltpu.VMEM((SWEEPS, targets, k, edge), f32),
            pltpu.VMEM((tpd, k, edge), f32),
            pltpu.VMEM((SWEEPS, 2 * n_grp, k // 2, 2 * k), f32),
            pltpu.VMEM((SWEEPS, max(sum(radices(n_rows // 2)), 1), k // 2, 2 * k), f32),
            pltpu.SemaphoreType.DMA((cap // UNROLL,)),
            pltpu.SemaphoreType.DMA((n_copies,)),
            pltpu.SemaphoreType.DMA((n_copies,)),
        ],
        compiler_params=pltpu.CompilerParams(
            collective_id=0, has_side_effects=True, vmem_limit_bytes=62 * 1024 * 1024
        ),
    )(meta, tiles, sketch.T)
    return basis.T


def solution(mesh):
    return jax.shard_map(
        local,
        mesh=mesh,
        in_specs=(
            P(("rows", "grp"), None, None),
            P(("rows", "grp"), None),
            P(("rows", "grp")),
            P(("rows", "grp"), None),
        ),
        out_specs=P(("rows", "grp"), None),
        check_vma=False,
    )
```

```python
import functools

import jax
import jax.numpy as jnp
from jax import lax
from jax.experimental import pallas as pl
from jax.experimental.pallas import tpu as pltpu
from jax.sharding import PartitionSpec as P

HIGHEST = lax.Precision.HIGHEST
MESH = pl.DeviceIdType.MESH
SWEEPS = 2
SUB = 4
UNROLL = 8
PIVOTS = 4


def radices(count):
    found = []
    while count > 1:
        radix = 4 if count % 4 == 0 else next(r for r in range(2, count + 1) if count % r == 0)
        found.append(radix)
        count //= radix
    return found


def dot(a, b):
    return jnp.dot(a, b, precision=HIGHEST, preferred_element_type=jnp.float32)


def dot_nt(a, b, precision=None):
    return lax.dot_general(
        a, b, (((1,), (1,)), ((), ())), precision=precision, preferred_element_type=jnp.float32
    )


def halves(x):
    high = x.astype(jnp.bfloat16)
    low = (x - high.astype(jnp.float32)).astype(jnp.bfloat16)
    return high, low


def quarters(x):
    rows, columns = x.shape[0] // 2, x.shape[1] // 2
    return x[:rows, :columns] + (
        (x[rows:, :columns] + x[:rows, columns:]) + x[rows:, columns:]
    )


def augmented(packed, k):
    half = k // 2
    lane = lax.broadcasted_iota(jnp.int32, (half, 2 * k), 1)
    row = lax.broadcasted_iota(jnp.int32, (half, 2 * k), 0)
    one = jnp.float32(1.0)
    zero = jnp.float32(0.0)
    top = jnp.where(lane >= k, pltpu.roll(packed, k, 1), jnp.where(lane == row, one, zero))
    low = jnp.where(lane >= k, packed, jnp.where(lane == row + half, one, zero))
    return jnp.concatenate([top, low], axis=0), jnp.ones((k, 2 * k), jnp.float32)


def eliminate(state, k, columns):
    m, pivots = state
    rows = lax.broadcasted_iota(jnp.int32, (k, 2 * k), 0)
    for j in columns:
        cols = [
            jnp.broadcast_to(m[:, k + j + i : k + j + i + 1], (k, 2 * k)) for i in range(PIVOTS)
        ]
        lines = [m[j + i : j + i + 1, :] for i in range(PIVOTS)]
        for i in range(PIVOTS):
            pivot = cols[i][j + i : j + i + 1, :]
            pivots = jnp.where(rows == j + i, pivot, pivots)
            factor = jnp.where(rows > j + i, cols[i] * (1.0 / pivot), 0.0)
            for n in range(i + 1, PIVOTS):
                lines[n] = lines[n] - factor[j + n : j + n + 1, :] * lines[i]
                cols[n] = cols[n] - factor * cols[i][j + n : j + n + 1, :]
            m = m - factor * lines[i]
    return m, pivots


def inverse_of(state, k):
    m, pivots = state
    return (m * lax.rsqrt(pivots))[:, :k]


def kernel(
    n_rows, n_grp, total_rows, meta, stored, sketch, out,
    tiles, t2, t3, run, part, rcv1, rcv2, rcv3, spr, img, gbuf, grest, load_sem, send_sem, recv_sem,
):
    cap, edge, _ = tiles.shape
    tpd, k, _ = img.shape
    half = k // 2
    n_hi = n_grp // 2
    block_tiles = n_grp * tpd
    width = tpd // SUB
    row = lax.axis_index("rows")
    grp = lax.axis_index("grp")
    lo = lax.rem(grp, 2)
    hi = grp // 2
    after = lax.rem(row + 1, n_rows)
    before = lax.rem(row + n_rows - 1, n_rows)
    core_peer = (row, hi * 2 + 1 - lo)

    def hi_peer(step):
        return lax.rem(hi + step, n_hi) * 2 + lo

    near_size = 2 * n_grp
    near_me = lax.rem(row, 2) * n_grp + grp

    def near_peer(step):
        at = lax.rem(near_me + step, near_size)
        return (row // 2 * 2 + at // n_grp, lax.rem(at, n_grp))

    rest = []
    stride = 2
    for radix in radices(n_rows // 2):
        digit = lax.rem(row // stride, radix)
        rest.append((radix, stride, digit))
        stride *= radix

    def rest_peer(stage, step):
        radix, stride, digit = rest[stage]
        return (row + (lax.rem(digit + step, radix) - digit) * stride, grp)

    def load(number):
        some = pl.ds(number * UNROLL, UNROLL)
        return pltpu.make_async_copy(stored.at[some], tiles.at[some], load_sem.at[number])

    for number in range(cap // UNROLL):
        load(number).start()

    peers = [(after, grp), (before, grp)]
    peers += [near_peer(s) for s in range(1, near_size)]
    for stage in range(len(rest)):
        peers += [rest_peer(stage, s) for s in range(1, rest[stage][0])]
    barrier = pltpu.get_barrier_semaphore()
    for peer in peers:
        pl.semaphore_signal(barrier, inc=1, device_id=peer, device_id_type=MESH)

    started = []

    def send(src, dst, peer):
        at = len(started)
        copy = pltpu.make_async_remote_copy(
            src_ref=src, dst_ref=dst, send_sem=send_sem.at[at], recv_sem=recv_sem.at[at],
            device_id=peer, device_id_type=MESH,
        )
        copy.start()
        started.append(copy)
        return copy

    def prev_of(s):
        return meta[s]

    def row_of(s):
        return meta[cap + s]

    def col_of(s):
        return meta[2 * cap + s]

    def last_of(t):
        return meta[3 * cap + t]

    run[0] = jnp.zeros((k, edge), jnp.float32)
    for t in range(tpd):
        img[t] = sketch[:, t * edge : (t + 1) * edge]

    def spread_sweep(first):
        def step(number, carry):
            base = number * UNROLL
            products = []
            if first:
                load(number).wait()
            for u in range(UNROLL):
                s = base + u
                if first:
                    t_high, t_low = halves(tiles[s])
                    t2[s, 0:edge, :] = t_high
                    t2[s, edge : 2 * edge, :] = t_low
                    wide = jnp.concatenate([t_high, t_low], axis=1)
                    t3[s] = wide
                else:
                    wide = t3[s]
                high, low = halves(img[jnp.maximum(row_of(s), 0)])
                products.append(
                    quarters(
                        jnp.dot(
                            jnp.concatenate([high, low], axis=0), wide,
                            preferred_element_type=jnp.float32,
                        )
                    )
                )
            for u in range(UNROLL):
                s = base + u
                run[s + 1] = products[u] + run[prev_of(s)]
            return carry

        lax.fori_loop(0, cap // UNROLL, step, 0)

    def image_sweep(it):
        for t in range(tpd):
            img[t] = jnp.zeros((k, edge), jnp.float32)

        def step(number, carry):
            base = number * UNROLL
            sums = [None] * tpd
            for u in range(UNROLL):
                s = base + u
                high, low = halves(spr[it, col_of(s)])
                product = quarters(dot_nt(jnp.concatenate([high, low], axis=0), t2[s]))
                at = row_of(s)
                for t in range(tpd):
                    term = jnp.where(at == t, jnp.float32(1.0), jnp.float32(0.0)) * product
                    sums[t] = term if sums[t] is None else sums[t] + term
            for t in range(tpd):
                img[t] = img[t] + sums[t]
            return carry

        lax.fori_loop(0, cap // UNROLL, step, 0)

    def gram_begin(it):
        total = None
        for t in range(tpd):
            tile = img[t]
            term = dot_nt(tile, jnp.concatenate([tile, tile], axis=0), HIGHEST)
            total = term if total is None else total + term
        lane = lax.broadcasted_iota(jnp.int32, (half, 2 * k), 1)
        gbuf[it, near_me] = jnp.where(lane < k, total[0:half], total[half:k])
        return [
            send(gbuf.at[it, near_me], gbuf.at[it, near_me], near_peer(s))
            for s in range(1, near_size)
        ]

    def gram_near(it, copies):
        for copy in copies:
            copy.wait_recv()
        total = gbuf[it, 0]
        for a in range(1, near_size):
            total = total + gbuf[it, a]
        return total

    def gram_rest_begin(it, stage, total):
        base = sum(r for r, _, _ in rest[:stage])
        radix, _, digit = rest[stage]
        grest[it, base + digit] = total
        return [
            send(grest.at[it, base + digit], grest.at[it, base + digit], rest_peer(stage, s))
            for s in range(1, radix)
        ]

    def gram_rest_end(it, stage, copies):
        base = sum(r for r, _, _ in rest[:stage])
        for copy in copies:
            copy.wait_recv()
        total = grest[it, base]
        for a in range(1, rest[stage][0]):
            total = total + grest[it, base + a]
        return total

    def gram_rest(it, total, copies):
        for stage in range(len(rest)):
            if copies is None:
                copies = gram_rest_begin(it, stage, total)
            total = gram_rest_end(it, stage, copies)
            copies = None
        return total

    def tiles_at(block, g, t=0):
        return block * block_tiles + g * tpd + t

    order = (0, 2, 1)

    def fill(it, block, g):
        def one(t, carry):
            at = tiles_at(block, g) + t
            part[it, at] = run[last_of(at)]
            return carry

        lax.fori_loop(0, tpd, one, 0)

    def scatter_core(it):
        copies = {}
        for block in order:
            for h in range(n_hi):
                g = h * 2 + 1 - lo
                fill(it, block, g)
                copies[block, h] = send(
                    part.at[it, pl.ds(tiles_at(block, g), tpd)],
                    rcv1.at[it, pl.ds((block * n_hi + h) * tpd, tpd)],
                    core_peer,
                )
        for block in order:
            for h in range(n_hi):
                fill(it, block, h * 2 + lo)
        return copies

    def scatter_hi(it, core_copies):
        copies = {}
        for block in order:
            for h in range(n_hi):
                core_copies[block, h].wait_recv()
            for step in range(1, n_hi):
                h = lax.rem(hi + step, n_hi)
                at = tiles_at(block, h * 2 + lo)
                from_core = (block * n_hi + h) * tpd
                for c in range(SUB - 1, -1, -1):
                    if (block, c) == (1, 0):
                        continue
                    mine = pl.ds(at + c * width, width)
                    part[it, mine] = part[it, mine] + rcv1[it, pl.ds(from_core + c * width, width)]
                    slot = (block * (n_hi - 1) + step - 1) * tpd + c * width
                    peer = (row, hi_peer(step))
                    if c == 0:
                        peer = (before if block == 0 else after, grp)
                    copies[block, step, c] = send(
                        part.at[it, mine], rcv2.at[it, pl.ds(slot, width)], peer
                    )
        return copies

    def scatter_late(it, copies):
        for step in range(1, n_hi):
            h = lax.rem(hi + step, n_hi)
            mine = pl.ds(tiles_at(1, h * 2 + lo), width)
            total = part[it, mine] + rcv1[it, pl.ds((n_hi + h) * tpd, width)]
            for block in (0, 2):
                copies[block, step, 0].wait_recv()
                slot = (block * (n_hi - 1) + step - 1) * tpd
                total = total + rcv2[it, pl.ds(slot, width)]
            part[it, mine] = total
            slot = (n_hi - 1 + step - 1) * tpd
            copies[1, step, 0] = send(
                part.at[it, mine], rcv2.at[it, pl.ds(slot, width)], (row, hi_peer(step))
            )

    def scatter_rows(it, hi_copies, blocks):
        copies = []
        for block in blocks:
            for c in range(SUB):
                mine = pl.ds(tiles_at(block, grp) + c * width, width)
                total = part[it, mine] + rcv1[
                    it, pl.ds((block * n_hi + hi) * tpd + c * width, width)
                ]
                for step in range(1, n_hi):
                    if block != 1 and c == 0:
                        continue
                    hi_copies[block, step, c].wait_recv()
                    slot = (block * (n_hi - 1) + step - 1) * tpd + c * width
                    total = total + rcv2[it, pl.ds(slot, width)]
                part[it, mine] = total
                if block == 0:
                    copies.append(
                        send(part.at[it, mine], rcv3.at[it, pl.ds(c * width, width)], (before, grp))
                    )
                if block == 2:
                    copies.append(
                        send(
                            part.at[it, mine],
                            rcv3.at[it, pl.ds(tpd + c * width, width)],
                            (after, grp),
                        )
                    )
        return copies

    def gather(it, row_copies, inverse):
        lead = []
        for c in range(SUB):
            row_copies[c].wait_recv()
            row_copies[SUB + c].wait_recv()
            for w in range(width):
                t = c * width + w
                value = part[it, tiles_at(1, grp) + t] + (rcv3[it, t] + rcv3[it, tpd + t])
                if inverse is not None:
                    value = dot(inverse, value)
                spr[it, tiles_at(1, grp) + t] = value

            def at(block, g, c=c):
                return spr.at[it, pl.ds(tiles_at(block, g) + c * width, width)]

            own = at(1, grp)
            up = send(own, at(0, grp), (after, grp))
            down = send(own, at(2, grp), (before, grp))
            across = [send(own, at(1, grp), (row, hi_peer(s))) for s in range(1, n_hi)]
            core = send(own, at(1, grp), core_peer)
            lead.append((up, down, across, core, at, c == 0))
        last = []
        later = []
        for up, down, across, core, at, first in lead:
            last.append(core)
            for block, copy in ((0, up), (2, down)):
                copy.wait_recv()
                piece = at(block, grp)
                for s in range(1, 1 if first else n_hi):
                    later.append((block, s, at, send(piece, piece, (row, hi_peer(s)))))
                last.append(send(piece, piece, core_peer))
            for s in range(1, n_hi):
                across[s - 1].wait_recv()
                source = hi_peer(n_hi - s)
                piece = at(1, source)
                if first:
                    later.append((0, s, at, send(piece, at(0, source), (after, grp))))
                    later.append((2, s, at, send(piece, at(2, source), (before, grp))))
                last.append(send(piece, piece, core_peer))
        for block, s, at, copy in later:
            copy.wait_recv()
            piece = at(block, hi_peer(n_hi - s))
            last.append(send(piece, piece, core_peer))
        for copy in last:
            copy.wait_recv()

    inverse = None
    near = None
    for it in range(SWEEPS):
        spread_sweep(it == 0)
        if it == 0:
            pl.semaphore_wait(barrier, len(peers))
        core_copies = scatter_core(it)
        far = None
        if near is not None:
            total = gram_near(it - 1, near)
            if rest:
                far = gram_rest_begin(it - 1, 0, total)
        hi_copies = scatter_hi(it, core_copies)
        if near is not None:
            state = augmented(gram_rest(it - 1, total, far), k)
            state = eliminate(state, k, range(0, k // 2, PIVOTS))
        row_copies = scatter_rows(it, hi_copies, order[:2])
        scatter_late(it, hi_copies)
        if near is not None:
            inverse = inverse_of(eliminate(state, k, range(k // 2, k, PIVOTS)), k)
        scatter_rows(it, hi_copies, order[2:])
        gather(it, row_copies, inverse)
        image_sweep(it)
        near = gram_begin(it)
    total = gram_rest(SWEEPS - 1, gram_near(SWEEPS - 1, near), None)
    state = eliminate(augmented(total, k), k, range(0, k, PIVOTS))
    inverse = inverse_of(state, k) * jnp.float32(total_rows**0.5)
    for t in range(tpd):
        out[:, t * edge : (t + 1) * edge] = dot(inverse, img[t])
    for copy in started:
        copy.wait_send()


def copies_of(n_rows, n_grp):
    n_hi = n_grp // 2
    scatter = 3 * n_hi + 3 * (n_hi - 1) * SUB + 2 * SUB
    gather = SUB * (2 + (n_hi - 1) + 1 + 2 * n_hi + 3 * (n_hi - 1))
    gram = 2 * n_grp - 1 + sum(r - 1 for r in radices(n_rows // 2))
    return SWEEPS * (scatter + gather + gram)


def local(tiles, coords, live, sketch):
    n_grp = lax.axis_size("grp")
    n_rows = lax.axis_size("rows")
    row = lax.axis_index("rows")
    grp = lax.axis_index("grp")
    cap, edge, _ = tiles.shape
    k = sketch.shape[1]
    tpd = sketch.shape[0] // edge
    block_tiles = n_grp * tpd
    targets = 3 * block_tiles
    slots = jnp.arange(cap, dtype=jnp.int32)
    used = slots < live[0]
    row_pos = coords[:, 0] - (row * block_tiles + grp * tpd)
    col_tiles = coords[:, 1]
    col_pos = (
        (col_tiles // block_tiles - row + 1 + n_rows) % n_rows * block_tiles
        + col_tiles % block_tiles
    )
    wanted = jnp.concatenate([col_pos, jnp.arange(targets, dtype=jnp.int32)])
    until = jnp.concatenate([slots, jnp.full((targets,), cap, jnp.int32)])
    same = (wanted[:, None] == col_pos[None, :]) & used[None, :] & (slots[None, :] < until[:, None])
    link = jnp.max(jnp.where(same, slots[None, :] + 1, 0), axis=1)
    meta = jnp.concatenate(
        [
            link[:cap],
            jnp.where(used, row_pos, -1),
            jnp.clip(col_pos, 0, targets - 1),
            link[cap:],
        ]
    )
    n_hi = n_grp // 2
    n_copies = copies_of(n_rows, n_grp)
    f32 = jnp.float32
    vmem = pl.BlockSpec(memory_space=pltpu.VMEM)
    basis = pl.pallas_call(
        functools.partial(kernel, n_rows, n_grp, n_rows * n_grp * sketch.shape[0]),
        out_shape=jax.ShapeDtypeStruct((k, tpd * edge), f32),
        in_specs=[
            pl.BlockSpec(memory_space=pltpu.SMEM), pl.BlockSpec(memory_space=pltpu.HBM), vmem,
        ],
        out_specs=vmem,
        scratch_shapes=[
            pltpu.VMEM((cap, edge, edge), f32),
            pltpu.VMEM((cap, 2 * edge, edge), jnp.bfloat16),
            pltpu.VMEM((cap, edge, 2 * edge), jnp.bfloat16),
            pltpu.VMEM((cap + 1, k, edge), f32),
            pltpu.VMEM((SWEEPS, targets, k, edge), f32),
            pltpu.VMEM((SWEEPS, 3 * n_hi * tpd, k, edge), f32),
            pltpu.VMEM((SWEEPS, 3 * max(n_hi - 1, 1) * tpd, k, edge), f32),
            pltpu.VMEM((SWEEPS, 2 * tpd, k, edge), f32),
            pltpu.VMEM((SWEEPS, targets, k, edge), f32),
            pltpu.VMEM((tpd, k, edge), f32),
            pltpu.VMEM((SWEEPS, 2 * n_grp, k // 2, 2 * k), f32),
            pltpu.VMEM((SWEEPS, max(sum(radices(n_rows // 2)), 1), k // 2, 2 * k), f32),
            pltpu.SemaphoreType.DMA((cap // UNROLL,)),
            pltpu.SemaphoreType.DMA((n_copies,)),
            pltpu.SemaphoreType.DMA((n_copies,)),
        ],
        compiler_params=pltpu.CompilerParams(
            collective_id=0, has_side_effects=True, vmem_limit_bytes=245 * 256 * 1024
        ),
    )(meta, tiles, sketch.T)
    return basis.T


def solution(mesh):
    return jax.shard_map(
        local,
        mesh=mesh,
        in_specs=(
            P(("rows", "grp"), None, None),
            P(("rows", "grp"), None),
            P(("rows", "grp")),
            P(("rows", "grp"), None),
        ),
        out_specs=P(("rows", "grp"), None),
        check_vma=False,
    )
```

```python
import functools

import jax
import jax.numpy as jnp
from jax import lax
from jax.experimental import pallas as pl
from jax.experimental.pallas import tpu as pltpu
from jax.sharding import PartitionSpec as P

HIGHEST = lax.Precision.HIGHEST
MESH = pl.DeviceIdType.MESH
SWEEPS = 2
SUB = 4
UNROLL = 8
PIVOTS = 8


def radices(count):
    found = []
    while count > 1:
        radix = 4 if count % 4 == 0 else next(r for r in range(2, count + 1) if count % r == 0)
        found.append(radix)
        count //= radix
    return found


def dot(a, b):
    return jnp.dot(a, b, precision=HIGHEST, preferred_element_type=jnp.float32)


def dot_nt(a, b, precision=None):
    return lax.dot_general(
        a, b, (((1,), (1,)), ((), ())), precision=precision, preferred_element_type=jnp.float32
    )


def halves(x):
    high = x.astype(jnp.bfloat16)
    low = (x - high.astype(jnp.float32)).astype(jnp.bfloat16)
    return high, low


def quarters(x):
    rows, columns = x.shape[0] // 2, x.shape[1] // 2
    return x[:rows, :columns] + (
        (x[rows:, :columns] + x[:rows, columns:]) + x[rows:, columns:]
    )


def augmented(packed, k):
    half = k // 2
    lane = lax.broadcasted_iota(jnp.int32, (half, 2 * k), 1)
    row = lax.broadcasted_iota(jnp.int32, (half, 2 * k), 0)
    one = jnp.float32(1.0)
    zero = jnp.float32(0.0)
    top = jnp.where(lane >= k, pltpu.roll(packed, k, 1), jnp.where(lane == row, one, zero))
    low = jnp.where(lane >= k, packed, jnp.where(lane == row + half, one, zero))
    return jnp.concatenate([top, low], axis=0), jnp.ones((k, 2 * k), jnp.float32)


def eliminate(state, k, columns):
    m, pivots = state
    rows = lax.broadcasted_iota(jnp.int32, (k, 2 * k), 0)
    for j in columns:
        cols = [
            jnp.broadcast_to(m[:, k + j + i : k + j + i + 1], (k, 2 * k)) for i in range(PIVOTS)
        ]
        lines = [m[j + i : j + i + 1, :] for i in range(PIVOTS)]
        for i in range(PIVOTS):
            pivot = cols[i][j + i : j + i + 1, :]
            pivots = jnp.where(rows == j + i, pivot, pivots)
            factor = jnp.where(rows > j + i, cols[i] * (1.0 / pivot), 0.0)
            for n in range(i + 1, PIVOTS):
                lines[n] = lines[n] - factor[j + n : j + n + 1, :] * lines[i]
                cols[n] = cols[n] - factor * cols[i][j + n : j + n + 1, :]
            m = m - factor * lines[i]
    return m, pivots


def inverse_of(state, k):
    m, pivots = state
    return (m * lax.rsqrt(pivots))[:, :k]


def kernel(
    n_rows, n_grp, total_rows, meta, stored, sketch, out,
    tiles, t2, t3, run, part, rcv1, rcv2, rcv3, spr, img, gbuf, grest, load_sem, send_sem, recv_sem,
):
    cap, edge, _ = tiles.shape
    tpd, k, _ = img.shape
    half = k // 2
    n_hi = n_grp // 2
    block_tiles = n_grp * tpd
    width = tpd // SUB
    row = lax.axis_index("rows")
    grp = lax.axis_index("grp")
    lo = lax.rem(grp, 2)
    hi = grp // 2
    after = lax.rem(row + 1, n_rows)
    before = lax.rem(row + n_rows - 1, n_rows)
    core_peer = (row, hi * 2 + 1 - lo)

    def hi_peer(step):
        return lax.rem(hi + step, n_hi) * 2 + lo

    near_size = 2 * n_grp
    near_me = lax.rem(row, 2) * n_grp + grp

    def near_peer(step):
        at = lax.rem(near_me + step, near_size)
        return (row // 2 * 2 + at // n_grp, lax.rem(at, n_grp))

    rest = []
    stride = 2
    for radix in radices(n_rows // 2):
        digit = lax.rem(row // stride, radix)
        rest.append((radix, stride, digit))
        stride *= radix

    def rest_peer(stage, step):
        radix, stride, digit = rest[stage]
        return (row + (lax.rem(digit + step, radix) - digit) * stride, grp)

    def load(number):
        some = pl.ds(number * UNROLL, UNROLL)
        return pltpu.make_async_copy(stored.at[some], tiles.at[some], load_sem.at[number])

    for number in range(cap // UNROLL):
        load(number).start()

    peers = [(after, grp), (before, grp)]
    peers += [near_peer(s) for s in range(1, near_size)]
    for stage in range(len(rest)):
        peers += [rest_peer(stage, s) for s in range(1, rest[stage][0])]
    barrier = pltpu.get_barrier_semaphore()
    for peer in peers:
        pl.semaphore_signal(barrier, inc=1, device_id=peer, device_id_type=MESH)

    started = []

    def send(src, dst, peer):
        at = len(started)
        copy = pltpu.make_async_remote_copy(
            src_ref=src, dst_ref=dst, send_sem=send_sem.at[at], recv_sem=recv_sem.at[at],
            device_id=peer, device_id_type=MESH,
        )
        copy.start()
        started.append(copy)
        return copy

    def prev_of(s):
        return meta[s]

    def row_of(s):
        return meta[cap + s]

    def col_of(s):
        return meta[2 * cap + s]

    def last_of(t):
        return meta[3 * cap + t]

    run[0] = jnp.zeros((k, edge), jnp.float32)
    for t in range(tpd):
        img[t] = sketch[:, t * edge : (t + 1) * edge]

    def spread_sweep(first):
        def step(number, carry):
            base = number * UNROLL
            products = []
            if first:
                load(number).wait()
            for u in range(UNROLL):
                s = base + u
                if first:
                    t_high, t_low = halves(tiles[s])
                    t2[s, 0:edge, :] = t_high
                    t2[s, edge : 2 * edge, :] = t_low
                    wide = jnp.concatenate([t_high, t_low], axis=1)
                    t3[s] = wide
                else:
                    wide = t3[s]
                high, low = halves(img[jnp.maximum(row_of(s), 0)])
                products.append(
                    quarters(
                        jnp.dot(
                            jnp.concatenate([high, low], axis=0), wide,
                            preferred_element_type=jnp.float32,
                        )
                    )
                )
            for u in range(UNROLL):
                s = base + u
                run[s + 1] = products[u] + run[prev_of(s)]
            return carry

        lax.fori_loop(0, cap // UNROLL, step, 0)

    def image_sweep(it):
        for t in range(tpd):
            img[t] = jnp.zeros((k, edge), jnp.float32)

        def step(number, carry):
            base = number * UNROLL
            sums = [None] * tpd
            for u in range(UNROLL):
                s = base + u
                high, low = halves(spr[it, col_of(s)])
                product = quarters(dot_nt(jnp.concatenate([high, low], axis=0), t2[s]))
                at = row_of(s)
                for t in range(tpd):
                    term = jnp.where(at == t, jnp.float32(1.0), jnp.float32(0.0)) * product
                    sums[t] = term if sums[t] is None else sums[t] + term
            for t in range(tpd):
                img[t] = img[t] + sums[t]
            return carry

        lax.fori_loop(0, cap // UNROLL, step, 0)

    def gram_begin(it):
        total = None
        for t in range(tpd):
            tile = img[t]
            term = dot_nt(tile, jnp.concatenate([tile, tile], axis=0), HIGHEST)
            total = term if total is None else total + term
        lane = lax.broadcasted_iota(jnp.int32, (half, 2 * k), 1)
        gbuf[it, near_me] = jnp.where(lane < k, total[0:half], total[half:k])
        return [
            send(gbuf.at[it, near_me], gbuf.at[it, near_me], near_peer(s))
            for s in range(1, near_size)
        ]

    def gram_near(it, copies):
        for copy in copies:
            copy.wait_recv()
        total = gbuf[it, 0]
        for a in range(1, near_size):
            total = total + gbuf[it, a]
        return total

    def gram_rest_begin(it, stage, total):
        base = sum(r for r, _, _ in rest[:stage])
        radix, _, digit = rest[stage]
        grest[it, base + digit] = total
        return [
            send(grest.at[it, base + digit], grest.at[it, base + digit], rest_peer(stage, s))
            for s in range(1, radix)
        ]

    def gram_rest_end(it, stage, copies):
        base = sum(r for r, _, _ in rest[:stage])
        for copy in copies:
            copy.wait_recv()
        total = grest[it, base]
        for a in range(1, rest[stage][0]):
            total = total + grest[it, base + a]
        return total

    def gram_rest(it, total, copies):
        for stage in range(len(rest)):
            if copies is None:
                copies = gram_rest_begin(it, stage, total)
            total = gram_rest_end(it, stage, copies)
            copies = None
        return total

    def tiles_at(block, g, t=0):
        return block * block_tiles + g * tpd + t

    order = (0, 2, 1)

    def fill(it, block, g):
        def one(t, carry):
            at = tiles_at(block, g) + t
            part[it, at] = run[last_of(at)]
            return carry

        lax.fori_loop(0, tpd, one, 0)

    def scatter_core(it):
        copies = {}
        for block in order:
            for h in range(n_hi):
                g = h * 2 + 1 - lo
                fill(it, block, g)
                copies[block, h] = send(
                    part.at[it, pl.ds(tiles_at(block, g), tpd)],
                    rcv1.at[it, pl.ds((block * n_hi + h) * tpd, tpd)],
                    core_peer,
                )
        for block in order:
            for h in range(n_hi):
                fill(it, block, h * 2 + lo)
        return copies

    def scatter_hi(it, core_copies):
        copies = {}
        for block in order:
            for h in range(n_hi):
                core_copies[block, h].wait_recv()
            for step in range(1, n_hi):
                h = lax.rem(hi + step, n_hi)
                at = tiles_at(block, h * 2 + lo)
                from_core = (block * n_hi + h) * tpd
                for c in range(SUB - 1, -1, -1):
                    if (block, c) == (1, 0):
                        continue
                    mine = pl.ds(at + c * width, width)
                    part[it, mine] = part[it, mine] + rcv1[it, pl.ds(from_core + c * width, width)]
                    slot = (block * (n_hi - 1) + step - 1) * tpd + c * width
                    peer = (row, hi_peer(step))
                    if c == 0:
                        peer = (before if block == 0 else after, grp)
                    copies[block, step, c] = send(
                        part.at[it, mine], rcv2.at[it, pl.ds(slot, width)], peer
                    )
        return copies

    def scatter_late(it, copies):
        for step in range(1, n_hi):
            h = lax.rem(hi + step, n_hi)
            mine = pl.ds(tiles_at(1, h * 2 + lo), width)
            total = part[it, mine] + rcv1[it, pl.ds((n_hi + h) * tpd, width)]
            for block in (0, 2):
                copies[block, step, 0].wait_recv()
                slot = (block * (n_hi - 1) + step - 1) * tpd
                total = total + rcv2[it, pl.ds(slot, width)]
            part[it, mine] = total
            slot = (n_hi - 1 + step - 1) * tpd
            copies[1, step, 0] = send(
                part.at[it, mine], rcv2.at[it, pl.ds(slot, width)], (row, hi_peer(step))
            )

    def scatter_rows(it, hi_copies, blocks):
        copies = []
        for block in blocks:
            for c in range(SUB):
                mine = pl.ds(tiles_at(block, grp) + c * width, width)
                total = part[it, mine] + rcv1[
                    it, pl.ds((block * n_hi + hi) * tpd + c * width, width)
                ]
                for step in range(1, n_hi):
                    if block != 1 and c == 0:
                        continue
                    hi_copies[block, step, c].wait_recv()
                    slot = (block * (n_hi - 1) + step - 1) * tpd + c * width
                    total = total + rcv2[it, pl.ds(slot, width)]
                part[it, mine] = total
                if block == 0:
                    copies.append(
                        send(part.at[it, mine], rcv3.at[it, pl.ds(c * width, width)], (before, grp))
                    )
                if block == 2:
                    copies.append(
                        send(
                            part.at[it, mine],
                            rcv3.at[it, pl.ds(tpd + c * width, width)],
                            (after, grp),
                        )
                    )
        return copies

    def gather(it, row_copies, inverse):
        lead = []
        for c in range(SUB):
            row_copies[c].wait_recv()
            row_copies[SUB + c].wait_recv()
            for w in range(width):
                t = c * width + w
                value = part[it, tiles_at(1, grp) + t] + (rcv3[it, t] + rcv3[it, tpd + t])
                if inverse is not None:
                    value = dot(inverse, value)
                spr[it, tiles_at(1, grp) + t] = value

            def at(block, g, c=c):
                return spr.at[it, pl.ds(tiles_at(block, g) + c * width, width)]

            own = at(1, grp)
            up = send(own, at(0, grp), (after, grp))
            down = send(own, at(2, grp), (before, grp))
            across = [send(own, at(1, grp), (row, hi_peer(s))) for s in range(1, n_hi)]
            core = send(own, at(1, grp), core_peer)
            lead.append((up, down, across, core, at, c == 0))
        last = []
        later = []
        for up, down, across, core, at, first in lead:
            last.append(core)
            for block, copy in ((0, up), (2, down)):
                copy.wait_recv()
                piece = at(block, grp)
                for s in range(1, 1 if first else n_hi):
                    later.append((block, s, at, send(piece, piece, (row, hi_peer(s)))))
                last.append(send(piece, piece, core_peer))
            for s in range(1, n_hi):
                across[s - 1].wait_recv()
                source = hi_peer(n_hi - s)
                piece = at(1, source)
                if first:
                    later.append((0, s, at, send(piece, at(0, source), (after, grp))))
                    later.append((2, s, at, send(piece, at(2, source), (before, grp))))
                last.append(send(piece, piece, core_peer))
        for block, s, at, copy in later:
            copy.wait_recv()
            piece = at(block, hi_peer(n_hi - s))
            last.append(send(piece, piece, core_peer))
        for copy in last:
            copy.wait_recv()

    inverse = None
    near = None
    for it in range(SWEEPS):
        spread_sweep(it == 0)
        if it == 0:
            pl.semaphore_wait(barrier, len(peers))
        core_copies = scatter_core(it)
        far = None
        if near is not None:
            total = gram_near(it - 1, near)
            if rest:
                far = gram_rest_begin(it - 1, 0, total)
        hi_copies = scatter_hi(it, core_copies)
        if near is not None:
            state = augmented(gram_rest(it - 1, total, far), k)
            state = eliminate(state, k, range(0, k // 2, PIVOTS))
        row_copies = scatter_rows(it, hi_copies, order[:2])
        scatter_late(it, hi_copies)
        if near is not None:
            inverse = inverse_of(eliminate(state, k, range(k // 2, k, PIVOTS)), k)
        scatter_rows(it, hi_copies, order[2:])
        gather(it, row_copies, inverse)
        image_sweep(it)
        near = gram_begin(it)
    total = gram_rest(SWEEPS - 1, gram_near(SWEEPS - 1, near), None)
    state = eliminate(augmented(total, k), k, range(0, k, PIVOTS))
    inverse = inverse_of(state, k) * jnp.float32(total_rows**0.5)
    for t in range(tpd):
        out[:, t * edge : (t + 1) * edge] = dot(inverse, img[t])
    for copy in started:
        copy.wait_send()


def copies_of(n_rows, n_grp):
    n_hi = n_grp // 2
    scatter = 3 * n_hi + 3 * (n_hi - 1) * SUB + 2 * SUB
    gather = SUB * (2 + (n_hi - 1) + 1 + 2 * n_hi + 3 * (n_hi - 1))
    gram = 2 * n_grp - 1 + sum(r - 1 for r in radices(n_rows // 2))
    return SWEEPS * (scatter + gather + gram)


def local(tiles, coords, live, sketch):
    n_grp = lax.axis_size("grp")
    n_rows = lax.axis_size("rows")
    row = lax.axis_index("rows")
    grp = lax.axis_index("grp")
    cap, edge, _ = tiles.shape
    k = sketch.shape[1]
    tpd = sketch.shape[0] // edge
    block_tiles = n_grp * tpd
    targets = 3 * block_tiles
    slots = jnp.arange(cap, dtype=jnp.int32)
    used = slots < live[0]
    row_pos = coords[:, 0] - (row * block_tiles + grp * tpd)
    col_tiles = coords[:, 1]
    col_pos = (
        (col_tiles // block_tiles - row + 1 + n_rows) % n_rows * block_tiles
        + col_tiles % block_tiles
    )
    wanted = jnp.concatenate([col_pos, jnp.arange(targets, dtype=jnp.int32)])
    until = jnp.concatenate([slots, jnp.full((targets,), cap, jnp.int32)])
    same = (wanted[:, None] == col_pos[None, :]) & used[None, :] & (slots[None, :] < until[:, None])
    link = jnp.max(jnp.where(same, slots[None, :] + 1, 0), axis=1)
    meta = jnp.concatenate(
        [
            link[:cap],
            jnp.where(used, row_pos, -1),
            jnp.clip(col_pos, 0, targets - 1),
            link[cap:],
        ]
    )
    n_hi = n_grp // 2
    n_copies = copies_of(n_rows, n_grp)
    f32 = jnp.float32
    vmem = pl.BlockSpec(memory_space=pltpu.VMEM)
    basis = pl.pallas_call(
        functools.partial(kernel, n_rows, n_grp, n_rows * n_grp * sketch.shape[0]),
        out_shape=jax.ShapeDtypeStruct((k, tpd * edge), f32),
        in_specs=[
            pl.BlockSpec(memory_space=pltpu.SMEM), pl.BlockSpec(memory_space=pltpu.HBM), vmem,
        ],
        out_specs=vmem,
        scratch_shapes=[
            pltpu.VMEM((cap, edge, edge), f32),
            pltpu.VMEM((cap, 2 * edge, edge), jnp.bfloat16),
            pltpu.VMEM((cap, edge, 2 * edge), jnp.bfloat16),
            pltpu.VMEM((cap + 1, k, edge), f32),
            pltpu.VMEM((SWEEPS, targets, k, edge), f32),
            pltpu.VMEM((SWEEPS, 3 * n_hi * tpd, k, edge), f32),
            pltpu.VMEM((SWEEPS, 3 * max(n_hi - 1, 1) * tpd, k, edge), f32),
            pltpu.VMEM((SWEEPS, 2 * tpd, k, edge), f32),
            pltpu.VMEM((SWEEPS, targets, k, edge), f32),
            pltpu.VMEM((tpd, k, edge), f32),
            pltpu.VMEM((SWEEPS, 2 * n_grp, k // 2, 2 * k), f32),
            pltpu.VMEM((SWEEPS, max(sum(radices(n_rows // 2)), 1), k // 2, 2 * k), f32),
            pltpu.SemaphoreType.DMA((cap // UNROLL,)),
            pltpu.SemaphoreType.DMA((n_copies,)),
            pltpu.SemaphoreType.DMA((n_copies,)),
        ],
        compiler_params=pltpu.CompilerParams(
            collective_id=0, has_side_effects=True, vmem_limit_bytes=245 * 256 * 1024
        ),
    )(meta, tiles, sketch.T)
    return basis.T


def solution(mesh):
    return jax.shard_map(
        local,
        mesh=mesh,
        in_specs=(
            P(("rows", "grp"), None, None),
            P(("rows", "grp"), None),
            P(("rows", "grp")),
            P(("rows", "grp"), None),
        ),
        out_specs=P(("rows", "grp"), None),
        check_vma=False,
    )
```
